256 devices in a mesh: wide: 32 (over x_lo, z, core), head: 8 (over y, x_hi).
Axes of the slice: x: 4 (x_hi: 2, x_lo: 2; x = x_hi * 2 + x_lo), y: 4, z: 8, core: 2. Of those that a mesh axis runs over, the one named last changes fastest.
Arguments:
- tokens: bfloat16 [32, 1024, 4096], P('wide'), may hold values from -6 to 6
- slab_index: int32 [32], P('wide'), may hold values from 0 to 3
- agg_query: bfloat16 [4096], P('head'), may hold values from -360 to 360
- agg_key_w: bfloat16 [4096, 4096], P('wide', 'head'), may hold values from -0.09375 to 0.09375
- agg_value_w: bfloat16 [4096, 4096], P('wide', 'head'), may hold values from -0.09375 to 0.09375
- agg_out_w: bfloat16 [4096, 4096], P('head', 'wide'), may hold values from -0.09375 to 0.09375
- norm_gain: float32 [4096], replicated, may hold values from 0.9 to 8
- query_w: bfloat16 [4096, 4096], P('wide', 'head'), may hold values from -0.09375 to 0.09375
- key_w: bfloat16 [4096, 4096], P('wide', 'head'), may hold values from -0.09375 to 0.09375
- value_w: bfloat16 [4096, 4096], P('wide', 'head'), may hold values from -0.09375 to 0.09375
Outputs:
- attended: bfloat16 [256, 4096], P('wide', 'head')
The draws below stay inside these ranges and needn't reach their ends.
All inputs are finite; a program needn't handle non-finite values.
Results may differ from the reference program's by a relative error of at most 0.035.
Values may be sent and summed in bfloat16 or wider, within the bound.
No kernel may reach another device: no remote copies, remote signals or barrier semaphores. Data moves between devices by JAX's collectives and lax.ppermute only.
A program may use at most 192 MiB of HBM per device.

```python
import math
import jax
import jax.numpy as jnp
from jax import lax

D = 4096
HEADS = 32
LOC_DEV = 32
Q_DEV = 8
VARS = 32
LOCS = 1024
SLAB = 256
N_WIDE = 32


def draw_agg_query(key, part):
    key = jax.random.fold_in(key, 11)
    base = jnp.clip(jax.random.normal(jax.random.fold_in(key, 1), (D,), jnp.float32), -6.0, 6.0)
    return base.astype(jnp.bfloat16)


def draw_norm_gain(key, part):
    key = jax.random.fold_in(key, 23)
    return 1.0 + 0.1 * jax.random.uniform(jax.random.fold_in(key, 2), (D,), jnp.float32, -1.0, 1.0)


def touch_ends(values, own_key, least, high):
    shape = values.shape
    spot = [jax.random.randint(jax.random.fold_in(own_key, axis), (), 0, shape[axis]) for axis in range(len(shape))]
    values = values.at[tuple(spot)].set(least)
    longest = shape.index(max(shape))
    spot[longest] = (spot[longest] + 1) % shape[longest]
    return values.at[tuple(spot)].set(high)


def shard_levels(stream_key, dims, shards, smallest, largest):
    def one(position, shards_of):
        heights = jax.random.uniform(jax.random.fold_in(jax.random.fold_in(stream_key, 6), position), (shards_of,), jnp.float32, smallest / len(shards), largest / len(shards))
        return jnp.repeat(jnp.exp(heights), dims[position] // shards_of).reshape((-1,) + (1,) * (len(dims) - position - 1))

    factor_of = one(*shards[0])
    for cut in shards[1:]:
        factor_of = factor_of * one(*cut)
    return factor_of


def bell_draw(key, extent, deviation, limit, pieces=(), kind=jnp.bfloat16):
    gain = shard_levels(key, extent, pieces, -0.22, 0.18) if pieces else 1.0
    drawn = jax.random.normal(key, extent, jnp.float32) * deviation * gain
    return jnp.minimum(jnp.maximum(drawn, -limit), limit).astype(kind)


def setup_inputs(seed: int = 0) -> dict:
    arg_keys = jax.random.split(jax.random.key(seed), 11)
    tokens = bell_draw(arg_keys[0], (VARS, LOCS, D), 1.0, 6.0, ((0, 32),))
    slab_index = touch_ends(jax.random.randint(arg_keys[1], (SLAB // Q_DEV,), 0, LOC_DEV // Q_DEV), jax.random.fold_in(arg_keys[1], 1), 0, (LOC_DEV // Q_DEV) - 1).astype(jnp.int32)
    agg_query = draw_agg_query(jax.random.fold_in(arg_keys[10], 71), 0)
    agg_key_w = bell_draw(arg_keys[3], (D, D), D ** -0.5, 0.09375, ((0, 32), (1, 8)))
    agg_value_w = bell_draw(arg_keys[4], (D, D), D ** -0.5, 0.09375, ((0, 32), (1, 8)))
    agg_out_w = bell_draw(arg_keys[5], (D, D), D ** -0.5, 0.09375, ((0, 8), (1, 32)))
    norm_gain = draw_norm_gain(jax.random.fold_in(arg_keys[10], 71), 0)
    query_w = bell_draw(arg_keys[7], (D, D), D ** -0.5, 0.09375, ((0, 32), (1, 8)))
    key_w = bell_draw(arg_keys[8], (D, D), D ** -0.5, 0.09375, ((0, 32), (1, 8)))
    value_w = bell_draw(arg_keys[9], (D, D), D ** -0.5, 0.09375, ((0, 32), (1, 8)))
    return dict(tokens=tokens, slab_index=slab_index, agg_query=agg_query, agg_key_w=agg_key_w, agg_value_w=agg_value_w, agg_out_w=agg_out_w, norm_gain=norm_gain, query_w=query_w, key_w=key_w, value_w=value_w)


def normalize(rows, norm_gain):
    values_f = rows.astype(jnp.float32)
    row_mean = lax.optimization_barrier(jnp.mean(values_f, axis=-1, keepdims=True))
    centred = values_f - row_mean
    row_var = lax.optimization_barrier(jnp.mean(centred * centred, axis=-1, keepdims=True))
    return (centred * lax.rsqrt(row_var + 1e-05) * norm_gain.astype(jnp.float32)).astype(jnp.bfloat16)

def take_block(block_rows, offset):
    return lax.dynamic_slice_in_dim(block_rows, offset, Q_DEV, 0)

def reference(tokens, slab_index, agg_query, agg_key_w, agg_value_w, agg_out_w, norm_gain, query_w, key_w, value_w):
    highest_precision = lax.Precision.HIGHEST
    head_dim = D // HEADS
    factor = 1.0 / math.sqrt(head_dim)
    token_floats = tokens.astype(jnp.float32)
    query_vec = agg_query.astype(jnp.float32).reshape(HEADS, head_dim)
    key_heads = agg_key_w.astype(jnp.float32).reshape(D, HEADS, head_dim)
    merged_heads_rows = jnp.einsum('dhj,hj->dh', key_heads, query_vec, precision=highest_precision) * factor
    aggregate_logits = jnp.einsum('wba,ak->wbk', token_floats, merged_heads_rows, precision=highest_precision)
    aggregate_probabilities = jax.nn.softmax(aggregate_logits, axis=0)
    pooled_tokens = jnp.einsum('ybz,ybw->bzw', aggregate_probabilities, token_floats, precision=highest_precision)
    value_heads = agg_value_w.astype(jnp.float32).reshape(D, HEADS, head_dim)
    head_out = jnp.einsum('lhd,dhj->lhj', pooled_tokens, value_heads, precision=highest_precision)
    agg_heads = head_out.reshape(LOCS, D).astype(jnp.bfloat16)
    aggregated = jnp.dot(agg_heads, agg_out_w, preferred_element_type=jnp.float32).astype(jnp.bfloat16)
    normed = normalize(aggregated, norm_gain)
    blocks = normed.reshape(N_WIDE, LOC_DEV, D)
    offsets = slab_index.astype(jnp.int32) * Q_DEV
    slab_rows = jax.vmap(take_block)(blocks, offsets).reshape(SLAB, D)
    queries = jnp.dot(slab_rows, query_w, preferred_element_type=jnp.float32).astype(jnp.bfloat16)
    key_proj = jnp.dot(normed, key_w, preferred_element_type=jnp.float32).astype(jnp.bfloat16)
    value_proj = jnp.dot(normed, value_w, preferred_element_type=jnp.float32).astype(jnp.bfloat16)
    query_f = queries.astype(jnp.float32).reshape(SLAB, HEADS, head_dim)
    key_f = key_proj.astype(jnp.float32).reshape(LOCS, HEADS, head_dim)
    value_f = value_proj.astype(jnp.float32).reshape(LOCS, HEADS, head_dim)
    scores = jnp.einsum('qhj,khj->hqk', query_f, key_f, precision=highest_precision) * factor
    probs = jax.nn.softmax(scores, axis=-1)
    attended = jnp.einsum('hqk,khj->qhj', probs, value_f, precision=highest_precision)
    return attended.reshape(SLAB, D).astype(jnp.bfloat16)
```

```python
import functools
import math

import jax
import jax.numpy as jnp
from jax import lax
from jax.experimental import pallas as pl
from jax.experimental.pallas import tpu as pltpu
from jax.sharding import Mesh, PartitionSpec as P

HEADS = 32
Q_DEV = 8
F32 = jnp.float32
BF16 = jnp.bfloat16
WIDE = ("xl", "z", "c")
HEAD = ("y", "xh")
LANES = 128
PARTS = 16
NT = (((1,), (1,)), ((), ()))
VMEM_BYTES = 48 * 1024 * 1024


def call(body, pos, out_shape, in_specs, out_specs, args, grid=(1,), scratch=(), flops=0, aliases=None):
    shapes = out_shape if isinstance(out_shape, (list, tuple)) else [out_shape]
    moved = sum(a.size * a.dtype.itemsize for a in args) + sum(math.prod(s.shape) * s.dtype.itemsize for s in shapes)
    return pl.pallas_call(
        body,
        out_shape=out_shape,
        grid_spec=pltpu.PrefetchScalarGridSpec(
            num_scalar_prefetch=1, grid=grid, in_specs=in_specs, out_specs=out_specs, scratch_shapes=list(scratch)
        ),
        input_output_aliases=aliases or {},
        compiler_params=pltpu.CompilerParams(vmem_limit_bytes=VMEM_BYTES),
        cost_estimate=pl.CostEstimate(flops=flops, bytes_accessed=moved, transcendentals=0),
    )(pos, *args)


def full(shape):
    return pl.BlockSpec(shape, lambda i, s: (0,) * len(shape))


def sds(shape, dtype):
    return jax.ShapeDtypeStruct(shape, dtype)


def lane(shape):
    return lax.broadcasted_iota(jnp.int32, shape, len(shape) - 1)


def rounded(x):
    return x.astype(BF16).astype(F32)


def pack_body(heads, factor, pos, q_ref, key_ref, value_ref, out_ref):
    columns = key_ref.shape[1]
    rows = key_ref.shape[0]
    head_dim = columns // heads
    row = lax.broadcasted_iota(jnp.int32, (PARTS, columns), 0)
    col = lane((PARTS, columns))
    q = jnp.broadcast_to(q_ref[...].astype(F32), (PARTS, columns))
    q_diag = jnp.where(lax.rem(row, heads) == lax.div(col, head_dim), q, 0.0).astype(BF16)
    merged = factor * lax.dot_general(q_diag, key_ref[...], NT, preferred_element_type=F32)
    hi = rounded(merged)
    mid = rounded(merged - hi)
    low = merged - hi - mid
    r = lax.broadcasted_iota(jnp.int32, merged.shape, 0)
    parts = jnp.where(r < heads, hi, jnp.where(r < 2 * heads, mid, jnp.where(r < 3 * heads, low, 0.0)))
    out_ref[:rows, :] = value_ref[...]
    out_ref[rows:, :] = jnp.concatenate([parts, jnp.zeros((PARTS, columns - rows), F32)], 1).astype(BF16)


def fold(x, heads):
    total = x + pltpu.roll(x, LANES - heads, 1) + pltpu.roll(x, LANES - 2 * heads, 1)
    return jnp.where(lane(x.shape) < heads, total, 0.0)


def unfold(s, heads):
    s = jnp.where(lane(s.shape) < heads, s, 0.0)
    hi = rounded(s)
    mid = rounded(s - hi)
    low = s - hi - mid
    return (hi + pltpu.roll(mid, heads, 1) + pltpu.roll(low, 2 * heads, 1)).astype(BF16)


def widen(p, heads, head_dim):
    return jnp.concatenate([jnp.broadcast_to(p[:, h : h + 1], (p.shape[0], head_dim)) for h in range(heads)], 1)


def merge(v0, s0, v1, s1, heads, head_dim):
    top = jnp.maximum(s0, s1)
    e0, e1 = jnp.exp(s0 - top), jnp.exp(s1 - top)
    total = e0 + e1
    v = widen(e0 / total, heads, head_dim) * v0 + widen(e1 / total, heads, head_dim) * v1.astype(F32)
    return v, top + jnp.log(total)


def value_body(n_chunks, first, last, heads, pos, *refs):
    tok = refs[: 4 * n_chunks]
    blocks = refs[4 * n_chunks : 6 * n_chunks]
    rest = refs[6 * n_chunks :]
    rows = tok[0].shape[1] if len(tok[0].shape) == 3 else tok[0].shape[0]
    d = tok[0].shape[-1]
    lhs = jnp.concatenate([t[...].reshape(rows, d) for t in tok], 1)
    pieces = [b[x] for i in range(n_chunks) for b in blocks[2 * i : 2 * i + 2] for x in (0, 1)]
    rhs = jnp.concatenate([p[:d] for p in pieces], 0)
    parts = jnp.concatenate([p[d:, :d] for p in pieces], 1)
    v = jnp.dot(lhs, rhs, preferred_element_type=F32)
    s = lax.dot_general(lhs, parts, NT, preferred_element_type=F32)
    s = jnp.concatenate([s, jnp.zeros((rows, LANES - PARTS), F32)], 1)
    if not first:
        v = v + rest[0][...]
        s = s + rest[1][...]
        rest = rest[2:]
    if not last:
        rest[0][...] = v
        rest[1][...] = s
        return
    msg_ref, v_ref, s_ref = rest
    groups, loc_dev, width = v_ref.shape
    s = fold(s, heads)
    v4 = v.reshape(groups, 2, loc_dev, width)
    s4 = s.reshape(groups, 2, loc_dev, LANES)
    p4 = unfold(s, heads).astype(F32).reshape(groups, 2, loc_dev, LANES)
    even = pos[0] == 0
    v_ref[...] = jnp.where(even, v4[:, 0], v4[:, 1])
    s_ref[...] = jnp.where(even, s4[:, 0], s4[:, 1])
    msg_ref[:, :, :width] = jnp.where(even, v4[:, 1], v4[:, 0]).astype(BF16)
    msg_ref[:, :, width:] = jnp.where(even, p4[:, 1], p4[:, 0]).astype(BF16)


def value_call(pos, toks, chunks, acc, last, heads, loc_dev, tile=256):
    locs, model = toks.shape
    n = len(chunks)
    width = chunks[0][1].shape[2]
    d = chunks[0][1].shape[1] - PARTS
    half = model // (2 * d)
    in_specs, args = [], []
    for slot, _, _ in chunks:
        for flip in (0, 1):
            for x in (0, 1):
                def place(i, s, slot=slot, flip=flip, x=x):
                    core = s[0] if flip == 0 else 1 - s[0]
                    return i, x * half + 2 * s[slot] + core
                in_specs.append(pl.BlockSpec((tile, d), place))
                args.append(toks)
    for _, own, other in chunks:
        in_specs += [full(own.shape)] * 2
        args += [own, other]
    rows2 = [pl.BlockSpec((tile, width), lambda i, s: (i, 0)), pl.BlockSpec((tile, LANES), lambda i, s: (i, 0))]
    aliases = None
    if acc is not None:
        if not last:
            aliases = {1 + len(args): 0, 2 + len(args): 1}
        in_specs += rows2
        args += list(acc)
    if last:
        g = tile // (2 * loc_dev)
        total = locs // (2 * loc_dev)
        shapes = [(total, loc_dev, width + LANES), (total, loc_dev, width), (total, loc_dev, LANES)]
        out_shape = [sds(sh, t) for sh, t in zip(shapes, (BF16, F32, F32))]
        out_specs = [pl.BlockSpec((g,) + sh[1:], lambda i, s: (i, 0, 0)) for sh in shapes]
    else:
        out_shape = [sds((locs, width), F32), sds((locs, LANES), F32)]
        out_specs = rows2
    body = functools.partial(value_body, n, acc is None, last, heads)
    flops = 2 * locs * 4 * n * d * width
    return call(body, pos, out_shape, in_specs, out_specs, args, grid=(locs // tile,), flops=flops, aliases=aliases)


def core_body(heads, pos, v_ref, s_ref, msg_ref, send_ref, v_out, s_out):
    width = v_ref.shape[-1]
    head_dim = width // heads
    for mine in (False, True):
        half = pos[1] if mine else 1 - pos[1]
        v, s = merge(
            v_ref[half],
            s_ref[half],
            msg_ref[half, :, :width],
            fold(msg_ref[half, :, width:].astype(F32), heads),
            heads,
            head_dim,
        )
        if mine:
            v_out[...] = v
            s_out[...] = s
        else:
            send_ref[:, :width] = v.astype(BF16)
            send_ref[:, width:] = unfold(s, heads)


def pair_body(heads, pos, v_ref, s_ref, msg_ref, out_ref):
    width = v_ref.shape[-1]
    s1 = fold(msg_ref[:, width:].astype(F32), heads)
    v, s = merge(v_ref[...], s_ref[...], msg_ref[:, :width], s1, heads, width // heads)
    out_ref[:, :width] = v.astype(BF16)
    out_ref[:, width:] = unfold(s, heads)


def ring_body(heads, pos, msg_ref, out_ref, scratch):
    n, rows, width = msg_ref.shape
    width -= LANES
    logs = [fold(msg_ref[i, :, width:].astype(F32), heads) for i in range(n)]
    top = functools.reduce(jnp.maximum, logs)
    powers = [jnp.exp(s - top) for s in logs]
    total = functools.reduce(jnp.add, powers)
    out = jnp.zeros((rows, width), F32)
    for i in range(n):
        out += widen(powers[i] / total, heads, width // heads) * msg_ref[i, :, :width].astype(F32)
    scratch[:rows, :] = out
    scratch[rows:, :] = out
    start = pl.multiple_of(pos[6] * Q_DEV, Q_DEV)
    out_ref[...] = scratch[pl.ds(start, rows), :].astype(BF16)


def out_body(pos, own_ref, far_ref, w_ref, out_ref, scratch):
    c, xl = pos[0], pos[1]
    for ref, side in ((own_ref, xl), (far_ref, 1 - xl)):
        scratch[2 * side + c] = ref[0]
        scratch[2 * side + 1 - c] = ref[1]
    rows = scratch.shape[0] * scratch.shape[1]
    a = scratch[...].reshape(rows, scratch.shape[2])
    n, _, width = w_ref.shape
    groups, per, _ = out_ref.shape
    for i in range(0, n, 2):
        w = jnp.concatenate([w_ref[i], w_ref[i + 1]], 1)
        got = jnp.dot(a, w, preferred_element_type=F32).astype(BF16)
        out_ref[:, :, i * width : (i + 2) * width] = got.reshape(groups, per, 2 * width)


def qkv_body(loc_dev, head_dim, pos, own_ref, y1_ref, y2_ref, y3_ref, w_ref, keep_ref, send_ref, scratch):
    c, y, xh = pos[0], pos[3], pos[4]
    for k, ref in enumerate((own_ref, y1_ref, y2_ref, y3_ref)):
        slot = 2 * lax.rem(y - k + 4, 4)
        scratch[slot + xh] = ref[0]
        scratch[slot + 1 - xh] = ref[1]
    _, per, model = scratch.shape
    scratch[8] = jnp.ones((per, model), BF16)
    a = scratch[...].reshape(9 * per, model)
    rows = 8 * per
    got = jnp.dot(a, w_ref[...], preferred_element_type=F32)
    columns = w_ref.shape[1] // 3
    a_f = a[:rows].astype(F32)
    mean = jnp.mean(a_f, axis=1, keepdims=True)
    dev = a_f - mean
    spread = jnp.sum(dev * dev, axis=1, keepdims=True)
    at = lane((rows, LANES))
    wide = jnp.where(at == 0, mean, jnp.where(at == 1, spread, jnp.where(at == 2, mean * mean, 0.0)))
    stats = jnp.transpose(wide)
    base = 2 * rows + 4 * Q_DEV

    def write(ref, x, h):
        for i in (0, 1):
            ref[x, i * rows : (i + 1) * rows, :] = got[:rows, i * columns + h * head_dim : i * columns + (h + 1) * head_dim]
        lo = 2 * columns + h * head_dim
        for w in range(4):
            ref[x, 2 * rows + w * Q_DEV : 2 * rows + (w + 1) * Q_DEV, :] = got[w * loc_dev : w * loc_dev + Q_DEV, lo : lo + head_dim]
        for i in range(3):
            lo = i * columns + h * head_dim
            ref[x, base + i : base + i + 1, :] = got[rows : rows + 1, lo : lo + head_dim]
        ref[x, base + 3 : base + 8, :] = stats[:5]

    for x in (0, 1):
        for core in (0, 1):
            @pl.when(c == core)
            def _():
                write(keep_ref, x, 2 * x + core)

            @pl.when(c != core)
            def _():
                write(send_ref, x, 2 * x + core)


def shift(x, axis, by):
    n = lax.axis_size(axis)
    return lax.ppermute(x, axis, [(i, (i + by) % n) for i in range(n)])


def ring_gather(x, axis, split):
    n = lax.axis_size(axis)
    got = [(0, x)]
    up = down = x
    for k in range(1, n // 2):
        up, down = shift(up, axis, 1), shift(down, axis, -1)
        got += [(n - k, up), (k, down)]
    half = x.shape[split] // 2
    first, second = jnp.split(up, [half], split)[0], jnp.split(down, [half], split)[1]
    got.append((n // 2, jnp.concatenate([shift(first, axis, 1), shift(second, axis, -1)], split)))
    return got


def by_bit(bit, mine, other):
    return jnp.where(bit == 0, jnp.stack([mine, other]), jnp.stack([other, mine]))


def pick(x, i):
    return lax.dynamic_index_in_dim(x, i, 0, keepdims=False)


def on_device(tokens, slab_index, agg_query, agg_key_w, agg_value_w, agg_out_w, norm_gain, query_w, key_w, value_w):
    model = tokens.shape[2]
    rows_w, columns = agg_key_w.shape
    head_dim = model // HEADS
    heads = columns // head_dim
    factor = 1.0 / math.sqrt(head_dim)
    n_z = lax.axis_size("z")
    locs = tokens.shape[1]
    loc_dev = locs // (4 * n_z)
    xl, z, c = lax.axis_index("xl"), lax.axis_index("z"), lax.axis_index("c")
    y, xh = lax.axis_index("y"), lax.axis_index("xh")
    wide = lax.axis_index(WIDE)
    toks = tokens.reshape(locs, model)
    zs = [lax.rem(z + k, n_z) for k in range(n_z)]
    pos = jnp.stack([c, xl, z, y, xh, wide, slab_index[0], *zs]).astype(jnp.int32)

    out_z = lax.all_gather(agg_out_w, "z", axis=0)
    packed = call(
        functools.partial(pack_body, heads, factor),
        pos,
        sds((rows_w + PARTS, columns), BF16),
        [full((1, columns)), full(agg_key_w.shape), full(agg_value_w.shape)],
        full((rows_w + PARTS, columns)),
        (agg_query.reshape(1, columns), agg_key_w, agg_value_w),
    )

    pair = by_bit(xl, packed, shift(packed, "xl", 1))
    gathered = [(7 + k, b, shift(b, "c", 1)) for k, b in ring_gather(pair, "z", 2)]
    acc = value_call(pos, toks, gathered[:1], None, False, heads, loc_dev)
    for i in range(1, n_z - 1, 2):
        acc = value_call(pos, toks, gathered[i : i + 2], acc, False, heads, loc_dev)
    msg, v, s = value_call(pos, toks, gathered[n_z - 1 :], acc, True, heads, loc_dev)

    msg = shift(msg, "c", 1)
    half = locs // 4
    tile = half // 2
    ext = columns + LANES
    wide_spec = lambda w: pl.BlockSpec((2, tile, w), lambda i, s: (0, i, 0))
    row_spec = lambda w: pl.BlockSpec((tile, w), lambda i, s: (i, 0))
    msg, v, s = call(
        functools.partial(core_body, heads),
        pos,
        [sds((half, ext), BF16), sds((half, columns), F32), sds((half, LANES), F32)],
        [wide_spec(columns), wide_spec(LANES), wide_spec(ext)],
        [row_spec(ext), row_spec(columns), row_spec(LANES)],
        (v.reshape(2, half, columns), s.reshape(2, half, LANES), msg.reshape(2, half, ext)),
        grid=(2,),
    )
    msg = shift(msg, "xl", 1)
    msg = call(
        functools.partial(pair_body, heads),
        pos,
        sds((half, ext), BF16),
        [row_spec(columns), row_spec(LANES), row_spec(ext)],
        row_spec(ext),
        (v, s, msg),
        grid=(2,),
    )
    msg = lax.all_to_all(msg.reshape(n_z, loc_dev, ext), "z", 0, 0, tiled=True)
    agg = call(
        functools.partial(ring_body, heads),
        pos,
        sds((loc_dev, columns), BF16),
        [full(msg.shape)],
        full((loc_dev, columns)),
        (msg,),
        scratch=[pltpu.VMEM((2 * loc_dev, columns), F32)],
    )

    near = jnp.stack([agg, shift(agg, "c", 1)])
    far = shift(near, "xl", 1)
    n_rows = 4 * loc_dev
    n_head = lax.axis_size(HEAD)
    part = n_z * rows_w
    partial_sum = call(
        out_body,
        pos,
        sds((n_head, n_rows // n_head, part), BF16),
        [full(near.shape), full(far.shape), full(out_z.shape)],
        full((n_head, n_rows // n_head, part)),
        (near, far, out_z),
        scratch=[pltpu.VMEM((4, loc_dev, columns), BF16)],
        flops=2 * n_rows * columns * part,
    )
    got = lax.all_to_all(partial_sum, HEAD, 0, 0, tiled=True)
    mine = jnp.sum(got.astype(F32), axis=0).astype(BF16)
    two = jnp.stack([mine, shift(mine, "xh", 1)])
    others = [shift(two, "y", k) for k in (1, 2, 3)]

    gain = lax.dynamic_slice_in_dim(norm_gain, wide * rows_w, rows_w, 0)[:, None]
    scaled = jnp.concatenate([(gain * w.astype(F32)).astype(BF16) for w in (key_w, value_w, query_w)], 1)
    qkv_w = lax.all_gather(scaled, "z", axis=0, tiled=True)
    base = 2 * n_rows + 4 * Q_DEV
    sums_shape = (2, base + 8, head_dim)
    keep, send = call(
        functools.partial(qkv_body, loc_dev, head_dim),
        pos,
        [sds(sums_shape, F32)] * 2,
        [full(two.shape)] * 4 + [full(qkv_w.shape)],
        [full(sums_shape)] * 2,
        (two, *others, qkv_w),
        scratch=[pltpu.VMEM((n_head + 1, n_rows // n_head, part), BF16)],
        flops=2 * n_rows * part * 3 * columns,
    )
    sums = keep + shift(send, "c", 1)
    sums = pick(sums, xl) + shift(pick(sums, 1 - xl), "xl", 1)
    col = sums[base : base + 3]
    mean_all = sums[base + 3] / 4
    between = sums[base + 5] / 4 - mean_all * mean_all
    var = sums[base + 4] / model + jnp.maximum(between, 0.0)
    rstd = lax.rsqrt(var + 1e-05)

    def normed(x, i, m, r):
        return ((x - m[:, None] * col[i][None, :]) * r[:, None]).astype(BF16)

    slab_of = lambda x: x.reshape(4, loc_dev)[:, :Q_DEV].reshape(-1)
    key_out = normed(sums[:n_rows], 0, mean_all, rstd)
    value_out = normed(sums[n_rows : 2 * n_rows], 1, mean_all, rstd)
    query_out = normed(sums[2 * n_rows : base], 2, slab_of(mean_all), slab_of(rstd))

    kv_all = jnp.concatenate([b for _, b in ring_gather(jnp.concatenate([key_out, value_out], 1), "z", 0)], 0)
    scores = factor * lax.dot_general(
        query_out, kv_all[:, :head_dim], (((1,), (1,)), ((), ())), preferred_element_type=F32
    )
    probs = jax.nn.softmax(scores, axis=-1)
    attended = jnp.dot(probs, kv_all[:, head_dim:].astype(F32), precision=lax.Precision.HIGHEST)
    att = attended.astype(BF16).reshape(2, 2, Q_DEV, head_dim)
    att = jnp.moveaxis(att, 1, 0)
    att = by_bit(c, pick(att, c), shift(pick(att, 1 - c), "c", 1))
    att = jnp.moveaxis(att, 1, 0)
    att = by_bit(xl, pick(att, xl), shift(pick(att, 1 - xl), "xl", 1))
    return jnp.moveaxis(att.reshape(heads, Q_DEV, head_dim), 1, 0).reshape(Q_DEV, columns)


def solution(mesh):
    n_z = mesh.devices.shape[0] // 4
    fine = Mesh(mesh.devices.reshape(2, n_z, 2, 4, 2), WIDE + HEAD)
    placed = (
        P(WIDE, None, None),
        P(WIDE),
        P(HEAD),
        P(WIDE, HEAD),
        P(WIDE, HEAD),
        P(HEAD, WIDE),
        P(),
        P(WIDE, HEAD),
        P(WIDE, HEAD),
        P(WIDE, HEAD),
    )
    return jax.shard_map(on_device, mesh=fine, in_specs=placed, out_specs=P(WIDE, HEAD), check_vma=False)
```

```python
import functools
import math

import jax
import jax.numpy as jnp
from jax import lax
from jax.experimental import pallas as pl
from jax.experimental.pallas import tpu as pltpu
from jax.sharding import Mesh, PartitionSpec as P

HEADS = 32
Q_DEV = 8
F32 = jnp.float32
BF16 = jnp.bfloat16
WIDE = ("xl", "z", "c")
HEAD = ("y", "xh")
LANES = 128
PARTS = 16
NT = (((1,), (1,)), ((), ()))
VMEM_BYTES = 44 * 1024 * 1024


def call(body, pos, out_shape, in_specs, out_specs, args, grid=(1,), scratch=(), cost=1, after=()):
    n_in, n_after = len(in_specs), len(after)
    kernel = body
    if n_after:
        kernel = lambda pos, *refs: body(pos, *refs[:n_in], *refs[n_in + n_after :])
    in_specs = list(in_specs) + [pl.BlockSpec(memory_space=pl.ANY)] * n_after
    return pl.pallas_call(
        kernel,
        out_shape=out_shape,
        grid_spec=pltpu.PrefetchScalarGridSpec(
            num_scalar_prefetch=1, grid=grid, in_specs=in_specs, out_specs=out_specs, scratch_shapes=list(scratch)
        ),
        compiler_params=pltpu.CompilerParams(vmem_limit_bytes=VMEM_BYTES),
        cost_estimate=pl.CostEstimate(flops=cost, bytes_accessed=1, transcendentals=0),
    )(pos, *args, *after)


def full(shape):
    return pl.BlockSpec(shape, lambda i, s: (0,) * len(shape))


def sds(shape, dtype):
    return jax.ShapeDtypeStruct(shape, dtype)


def lane(shape):
    return lax.broadcasted_iota(jnp.int32, shape, len(shape) - 1)


def rounded(x):
    return x.astype(BF16).astype(F32)


def side_by_side(blocks):
    total = sum(b.shape[1] for b in blocks)
    col = lax.broadcasted_iota(jnp.int32, (blocks[0].shape[0], total), 1)
    out, start = None, 0
    for b in blocks:
        here = jnp.pad(b, ((0, 0), (start, total - start - b.shape[1])))
        out = here if out is None else jnp.where(col >= start, here, out)
        start += b.shape[1]
    return out


def same_body(*refs):
    pass


def once(x, after):
    anywhere = pl.BlockSpec(memory_space=pl.ANY)
    return pl.pallas_call(
        same_body,
        out_shape=sds(x.shape, x.dtype),
        in_specs=[anywhere] * 2,
        out_specs=anywhere,
        input_output_aliases={0: 0},
        cost_estimate=pl.CostEstimate(flops=1, bytes_accessed=1, transcendentals=0),
    )(x, after)


def split3(x):
    hi = lax.reduce_precision(x, 8, 7)
    mid = lax.reduce_precision(x - hi, 8, 7)
    low = lax.reduce_precision(x - hi - mid, 8, 7)
    return hi.astype(BF16), mid.astype(BF16), low.astype(BF16)


def fold(x, heads):
    total = x + pltpu.roll(x, LANES - heads, 1) + pltpu.roll(x, LANES - 2 * heads, 1)
    return jnp.where(lane(x.shape) < heads, total, 0.0)


def unfold(s, heads):
    s = jnp.where(lane(s.shape) < heads, s, 0.0)
    hi = rounded(s)
    mid = rounded(s - hi)
    low = s - hi - mid
    return (hi + pltpu.roll(mid, heads, 1) + pltpu.roll(low, 2 * heads, 1)).astype(BF16)


def pack_rows(s, heads):
    parts = unfold(s, heads).astype(F32)
    n = s.shape[0] // 4
    packed = parts[:n]
    for q in (1, 2, 3):
        packed = packed + pltpu.roll(parts[q * n : (q + 1) * n], q * LANES // 4, 1)
    return jnp.concatenate([packed[q * n // 4 : (q + 1) * n // 4] for q in range(4)], 1).astype(BF16)


def unpack_rows(rows, heads):
    rows = rows.astype(F32)
    packed = jnp.concatenate([rows[:, q * LANES : (q + 1) * LANES] for q in range(4)], 0)
    return jnp.concatenate([fold(packed if q == 0 else pltpu.roll(packed, LANES - q * LANES // 4, 1), heads) for q in range(4)], 0)


def widen(p, heads, head_dim):
    return jnp.concatenate([jnp.broadcast_to(p[:, h : h + 1], (p.shape[0], head_dim)) for h in range(heads)], 1)


def merge(v0, s0, v1, s1, heads, head_dim):
    top = jnp.maximum(s0, s1)
    e0, e1 = jnp.exp(s0 - top), jnp.exp(s1 - top)
    total = e0 + e1
    v = widen(e0 / total, heads, head_dim) * v0 + widen(e1 / total, heads, head_dim) * v1.astype(F32)
    return v, top + jnp.log(total)


def value_body(pieces, n_tok, n_blocks, first, last, heads, pos, *refs):
    toks = refs[:n_tok]
    blocks = refs[n_tok : n_tok + n_blocks]
    rest = refs[n_tok + n_blocks :]
    rows, d = toks[0].shape[0], toks[0].shape[1] // 2
    lhs, rhs, parts = [], [], []
    for tok, flip, block, place in pieces:
        core = pos[0] if flip == 0 else 1 - pos[0]
        lhs.append(toks[tok][:, pl.ds(pl.multiple_of(core * d, d), d)])
        rhs.append(blocks[block][place, :d, :])
        parts.append(blocks[block][place, d:, :d])
    lhs = jnp.concatenate(lhs, 1)
    v = jnp.dot(lhs, jnp.concatenate(rhs, 0), preferred_element_type=F32)
    s = lax.dot_general(lhs, jnp.concatenate(parts, 1), NT, preferred_element_type=F32)
    s = jnp.concatenate([s, jnp.zeros((rows, LANES - PARTS), F32)], 1)
    if not first:
        v = v + rest[0][...]
        s = s + rest[1][...]
        rest = rest[2:]
    if not last:
        rest[0][...] = v
        rest[1][...] = s
        return
    msg_ref, v_ref, s_ref = rest
    groups, loc_dev, width = v_ref.shape
    s = fold(s, heads)
    v4 = v.reshape(groups, 2, loc_dev, width)
    s4 = s.reshape(groups, 2, loc_dev, LANES)
    p4 = unfold(s, heads).astype(F32).reshape(groups, 2, loc_dev, LANES)
    even = pos[0] == 0
    v_ref[...] = jnp.where(even, v4[:, 0], v4[:, 1])
    s_ref[...] = jnp.where(even, s4[:, 0], s4[:, 1])
    msg_ref[:, :, :width] = jnp.where(even, v4[:, 1], v4[:, 0]).astype(BF16)
    msg_ref[:, :, width:] = jnp.where(even, p4[:, 1], p4[:, 0]).astype(BF16)


def value_call(pos, toks, chunks, acc, last, heads, loc_dev, mine, after=(), tile=512):
    locs, model = toks.shape[0] // 2, toks.shape[1]
    arrays, pieces, in_specs, args = [], [], [], []
    for offset, blocks in chunks:
        for x in (0, 1):
            def place(i, s, offset=offset, x=x):
                side = s[1] if x == 0 else 1 - s[1]
                half = s[1] if mine else 1 - s[1]
                return half * (locs // tile) + i, side * (model // 512) + s[7 + offset]
            in_specs.append(pl.BlockSpec((tile, 256), place))
            args.append(toks)
            for flip in (0, 1):
                array, at = blocks[x][flip]
                found = [i for i, o in enumerate(arrays) if o is array]
                if not found:
                    arrays.append(array)
                pieces.append((len(args) - 1, flip, found[0] if found else len(arrays) - 1, at))
    n_tok = len(args)
    in_specs += [full(o.shape) for o in arrays]
    args += arrays
    width = arrays[0].shape[2]
    rows2 = [pl.BlockSpec((tile, width), lambda i, s: (i, 0)), pl.BlockSpec((tile, LANES), lambda i, s: (i, 0))]
    if acc is not None:
        in_specs += rows2
        args += list(acc)
    if last:
        g = tile // (2 * loc_dev)
        total = locs // (2 * loc_dev)
        shapes = [(total, loc_dev, width + LANES), (total, loc_dev, width), (total, loc_dev, LANES)]
        out_shape = [sds(sh, t) for sh, t in zip(shapes, (BF16, F32, F32))]
        out_specs = [pl.BlockSpec((g,) + sh[1:], lambda i, s: (i, 0, 0)) for sh in shapes]
    else:
        out_shape = [sds((locs, width), F32), sds((locs, LANES), F32)]
        out_specs = rows2
    body = functools.partial(value_body, pieces, n_tok, len(arrays), acc is None, last, heads)
    return call(body, pos, out_shape, in_specs, out_specs, args, grid=(locs // tile,), after=after)


def stack_body(pos, *refs):
    for i, ref in enumerate(refs[:-1]):
        refs[-1][i] = ref[...]


def side_body(pos, left_ref, right_ref, out_ref):
    width = left_ref.shape[1]
    out_ref[0, :, :width] = left_ref[...]
    out_ref[0, :, width:] = right_ref[...]


def join_body(pos, *refs):
    start = 0
    for ref in refs[:-1]:
        refs[-1][start : start + ref.shape[0]] = ref[...]
        start += ref.shape[0]


def first_body(heads, pos, v_ref, s_ref, msg_ref, out_ref):
    rows, width = v_ref.shape
    s1 = fold(msg_ref[:, width:].astype(F32), heads)
    v, s = merge(v_ref[...], s_ref[...], msg_ref[:, :width], s1, heads, width // heads)
    out_ref[:rows, :] = v.astype(BF16)
    out_ref[rows:, :] = pack_rows(s, heads)


def last_body(heads, pos, v_ref, s_ref, far_ref, top_ref, bottom_ref, out_ref):
    width = v_ref.shape[-1]
    rows = v_ref.shape[0]
    near = jnp.concatenate([top_ref[...], bottom_ref[...]], 0)
    logs = [s_ref[...], unpack_rows(far_ref[rows:, :], heads), fold(near[:, width:].astype(F32), heads)]
    values = [v_ref[...], far_ref[:rows, :].astype(F32), near[:, :width].astype(F32)]
    top = functools.reduce(jnp.maximum, logs)
    powers = [jnp.exp(x - top) for x in logs]
    total = functools.reduce(jnp.add, powers)
    v = sum(widen(p / total, heads, width // heads) * x for p, x in zip(powers, values))
    out_ref[:, :width] = v.astype(BF16)
    out_ref[:, width:] = unfold(top + jnp.log(total), heads)


def pair_call(pos, v, s, msg, heads, to_send, after=()):
    rows, width = v.shape
    tile = rows // 2
    specs = [pl.BlockSpec((tile, w), lambda i, s: (i, 0)) for w in (width, LANES, width + LANES)]
    if to_send:
        out, out_specs = sds(msg.shape, BF16), specs[2]
    else:
        out, out_specs = [sds(v.shape, F32), sds(s.shape, F32)], specs[:2]
    return call(functools.partial(pair_body, heads), pos, out, specs, out_specs, (v, s, msg), grid=(2,), after=after)


def ring_body(heads, pos, msg_ref, out_ref, scratch):
    n, rows, width = msg_ref.shape
    width -= LANES
    logs = [fold(msg_ref[i, :, width:].astype(F32), heads) for i in range(n)]
    top = functools.reduce(jnp.maximum, logs)
    powers = [jnp.exp(s - top) for s in logs]
    total = functools.reduce(jnp.add, powers)
    out = jnp.zeros((rows, width), F32)
    for i in range(n):
        out += widen(powers[i] / total, heads, width // heads) * msg_ref[i, :, :width].astype(F32)
    scratch[:rows, :] = out
    scratch[rows:, :] = out
    start = pl.multiple_of(pos[6] * Q_DEV, Q_DEV)
    out_ref[...] = scratch[pl.ds(start, rows), :].astype(BF16)


def out_body(pos, own_ref, far_ref, w_ref, *refs):
    outs, scratch, result = refs[:-2], refs[-2], refs[-1]
    c, xl, y = pos[0], pos[1], pos[3]
    for ref, side in ((own_ref, xl), (far_ref, 1 - xl)):
        scratch[2 * side + c] = ref[0]
        scratch[2 * side + 1 - c] = ref[1]
    groups, per, _ = scratch.shape
    a = scratch[...].reshape(groups * per, scratch.shape[2])
    width = LANES
    quarters = w_ref.shape[1] // width

    def weights(i):
        rows = w_ref[i * width : (i + 1) * width, :]
        return jnp.concatenate([rows[:, q * width : (q + 1) * width] for q in range(quarters)], 0)

    for i in range(0, w_ref.shape[0] // width, 2):
        w = jnp.concatenate([weights(i), weights(i + 1)], 1)
        got = jnp.dot(a, w, preferred_element_type=F32).astype(BF16)
        result[:, :, i * width : (i + 2) * width] = got.reshape(groups, per, 2 * width)
    for k, ref in enumerate(outs):
        ref[...] = result[lax.bitwise_xor(y, k)]


def qkv_body(loc_dev, head_dim, pos, own_ref, y1_ref, y2_ref, y3_ref, gain_ref, w_ref, keep_ref, send_ref, scratch):
    c, y = pos[0], pos[3]
    for k, ref in enumerate((own_ref, y1_ref, y2_ref, y3_ref)):
        scratch[lax.bitwise_xor(y, k)] = ref[...]
    groups, per, model = scratch.shape
    rows = groups * per
    columns = w_ref.shape[1] // 3
    start = pl.multiple_of(c * LANES, LANES)
    gain = gain_ref[0, :, pl.ds(start, LANES)]
    gain = jnp.concatenate([gain[i : i + 1] for i in range(gain.shape[0])], 1)
    hi = rounded(gain)
    mid = rounded(gain - hi)
    row = lax.broadcasted_iota(jnp.int32, (16, model), 0)
    extra = jnp.where(row == 0, hi, jnp.where(row == 1, mid, jnp.where(row == 2, gain - hi - mid, 0.0)))
    a_f = scratch[...].reshape(rows, model).astype(F32)
    mean = jnp.mean(a_f, axis=1, keepdims=True)
    dev = a_f - mean
    spread = jnp.sum(dev * dev, axis=1, keepdims=True)
    lhs = jnp.concatenate([(dev * gain).astype(BF16), extra.astype(BF16)], 0)
    got = jnp.dot(lhs, w_ref[...], preferred_element_type=F32)
    column_sums = got[rows : rows + 1] + got[rows + 1 : rows + 2] + got[rows + 2 : rows + 3]
    got = got[:rows] + mean * column_sums
    at = lane((rows, LANES))
    wide = jnp.where(at == 0, mean, jnp.where(at == 1, spread, jnp.where(at == 2, mean * mean, 0.0)))
    stats = jnp.transpose(wide)
    base = 2 * rows + 4 * Q_DEV

    def write(ref, x, h):
        for i in (0, 1):
            ref[x, i * rows : (i + 1) * rows, :] = got[:rows, i * columns + h * head_dim : i * columns + (h + 1) * head_dim]
        lo = 2 * columns + h * head_dim
        for w in range(4):
            ref[x, 2 * rows + w * Q_DEV : 2 * rows + (w + 1) * Q_DEV, :] = got[w * loc_dev : w * loc_dev + Q_DEV, lo : lo + head_dim]
        for i in range(3):
            lo = i * columns + h * head_dim
            ref[x, base + i : base + i + 1, :] = column_sums[:, lo : lo + head_dim]
        ref[x, base + 3 : base + 8, :] = stats[:5]

    for x in (0, 1):
        for core in (0, 1):
            @pl.when(c == core)
            def _():
                write(keep_ref, x, 2 * x + core)

            @pl.when(c != core)
            def _():
                write(send_ref, x, 2 * x + core)


def shift(x, axis, by):
    n = lax.axis_size(axis)
    return lax.ppermute(x, axis, [(i, (i + by) % n) for i in range(n)])


def flip(x, axis, bits):
    return lax.ppermute(x, axis, [(i, i ^ bits) for i in range(lax.axis_size(axis))])


def by_bit(bit, mine, other):
    return jnp.where(bit == 0, jnp.stack([mine, other]), jnp.stack([other, mine]))


def pick(x, i):
    return lax.dynamic_index_in_dim(x, i, 0, keepdims=False)


def on_device(tokens, slab_index, agg_query, agg_key_w, agg_value_w, agg_out_w, norm_gain, query_w, key_w, value_w):
    model = tokens.shape[2]
    rows_w, columns = agg_key_w.shape
    head_dim = model // HEADS
    heads = columns // head_dim
    factor = 1.0 / math.sqrt(head_dim)
    n_z = lax.axis_size("z")
    locs = tokens.shape[1]
    loc_dev = locs // (4 * n_z)
    xl, z, c = lax.axis_index("xl"), lax.axis_index("z"), lax.axis_index("c")
    y, xh = lax.axis_index("y"), lax.axis_index("xh")
    wide = lax.axis_index(WIDE)
    toks = tokens.reshape(locs, model)
    zs = [lax.rem(z + k, n_z) for k in range(n_z)]
    pos = jnp.stack([c, xl, z, y, xh, wide, slab_index[0], *zs]).astype(jnp.int32)

    out_blocks = [agg_out_w[i : i + rows_w] for i in range(0, columns, rows_w)]
    later = side_by_side([key_w, value_w, query_w, *out_blocks])

    own_head = jnp.arange(columns)[None, :] // head_dim == jnp.arange(heads)[:, None]
    q_diag = jnp.where(own_head, agg_query[None, :], 0).astype(BF16)
    merged = factor * lax.dot_general(q_diag, agg_key_w, NT, preferred_element_type=F32)
    parts = jnp.concatenate([*split3(merged), jnp.zeros((PARTS - 3 * heads, rows_w), BF16)], 0)
    packed = jnp.concatenate([agg_value_w, jnp.pad(parts, ((0, 0), (0, columns - rows_w)))], 0)

    def stack(blocks, axis, after):
        if axis:
            shape = blocks[0].shape[:1] + (columns,)
            return call(side_body, pos, sds((1,) + shape, BF16), [full(b.shape) for b in blocks], full((1,) + shape), blocks, after=after)
        shape = (len(blocks),) + blocks[0].shape
        return call(stack_body, pos, sds(shape, BF16), [full(b.shape) for b in blocks], full(shape), blocks, after=after)

    at = {}

    def join(lot, after=()):
        shape = (sum(b.shape[0] for b in lot),) + packed.shape
        return call(join_body, pos, sds(shape, BF16), [full(b.shape) for b in lot], full(shape), lot, after=after)

    def over_cores(lot, joined):
        swapped = shift(joined, "c", 1)
        start = 0
        for block in lot:
            at[id(block)] = (swapped, start)
            start += block.shape[0]
        return swapped

    ups, downs, owns, fars = [packed], [packed], [packed[None]], [shift(packed[None], "xl", 1)]
    lots, joins = [], []
    for k in range(1, n_z // 2):
        ups.append(shift(ups[-1], "z", 1))
        downs.append(shift(downs[-1], "z", -1))
        if k == 3:
            lots.append([owns[0], fars[0], owns[1], fars[1]])
            joins.append(join(lots[0]))
        owns.append(stack((ups[-1], downs[-1]), 0, [*fars[-1:], *([later] if k == 1 else joins)]))
        fars.append(shift(owns[-1], "xl", 1))
    first = shift(ups[-1][:, : columns // 2], "z", 1)
    second = shift(downs[-1][:, columns // 2 :], "z", -1)
    lots.append([owns[2], fars[2], owns[3]])
    joins.append(join(lots[1]))
    over_cores(lots[0], joins[0])
    owns.append(stack((first, second), 1, [fars[-1], joins[1], at[id(owns[0])][0]]))
    over_cores(lots[1], joins[1])
    fars.append(shift(owns[-1], "xl", 1))
    weights_z = lax.all_gather(once(later, owns[2]), "z", axis=0, tiled=True)

    def chunk(offset, k, i):
        rows = []
        for block in (owns[k], fars[k]):
            other, start = at[id(block)]
            rows.append([(block, i), (other, start + i)])
        return offset, rows

    chunks = [chunk(0, 0, 0)]
    for k in (1, 2):
        chunks += [chunk(n_z - k, k, 0), chunk(k, k, 1)]
    acc = value_call(pos, toks, chunks, None, False, heads, loc_dev, False)
    lot = [fars[3], owns[4], fars[4]]
    over_cores(lot, join(lot, after=acc[1:]))
    chunks += [chunk(n_z - 3, 3, 0), chunk(3, 3, 1), chunk(4, 4, 0)]

    half = locs // 4
    ext = columns + LANES
    flat = lambda x: x.reshape(half, x.shape[-1])
    msg, v, s = value_call(pos, toks, chunks[5:], acc, True, heads, loc_dev, False)
    args = (flat(v), flat(s), flat(shift(msg, "c", 1)))
    shape = (half + half // 16, columns)
    gone = call(functools.partial(first_body, heads), pos, sds(shape, BF16), [full(a.shape) for a in args], full(shape), args)
    far_msg = shift(gone, "xl", 1)
    msg, v, s = value_call(pos, toks, chunks, None, True, heads, loc_dev, True, after=(gone,))
    two = [x.reshape(half // 2, ext) for x in (shift(msg[: n_z // 2], "c", 1), shift(msg[n_z // 2 :], "c", 1))]
    args = (flat(v), flat(s), far_msg, *two)
    msg = call(functools.partial(last_body, heads), pos, sds((half, ext), BF16), [full(a.shape) for a in args], full((half, ext)), args)
    msg = lax.all_to_all(msg.reshape(n_z, loc_dev, ext), "z", 0, 0, tiled=True)
    agg = call(
        functools.partial(ring_body, heads),
        pos,
        sds((loc_dev, columns), BF16),
        [full(msg.shape)],
        full((loc_dev, columns)),
        (msg,),
        scratch=[pltpu.VMEM((2 * loc_dev, columns), F32)],
    )

    near = jnp.stack([agg, shift(agg, "c", 1)])
    far = shift(near, "xl", 1)
    n_rows = 4 * loc_dev
    part = n_z * rows_w
    block = (loc_dev, part)
    sent = call(
        out_body,
        pos,
        [sds(block, BF16)] * 4,
        [full(near.shape), full(far.shape), full((part, columns))],
        [full(block)] * 4,
        (near, far, weights_z[:, 3 * columns :]),
        scratch=[pltpu.VMEM((4, loc_dev, columns), BF16), pltpu.VMEM((4,) + block, BF16)],
    )
    got = [flip(sent[k], "y", k) for k in (1, 2, 3)]
    mine = sum(x.astype(F32) for x in (sent[0], *got))
    mine = (mine + shift(mine.astype(BF16), "xh", 1).astype(F32)).astype(BF16)
    others = [flip(mine, "y", k) for k in (1, 2, 3)]

    base = 2 * n_rows + 4 * Q_DEV
    sums_shape = (2, base + 8, head_dim)
    keep, send = call(
        functools.partial(qkv_body, loc_dev, head_dim),
        pos,
        [sds(sums_shape, F32)] * 2,
        [full(mine.shape)] * 4
        + [pl.BlockSpec((1, n_z, 2 * rows_w), lambda i, s: (s[1], 0, 0))]
        + [full((part, 3 * columns))],
        [full(sums_shape)] * 2,
        (mine, *others, norm_gain.reshape(2, n_z, 2 * rows_w), weights_z[:, : 3 * columns]),
        scratch=[pltpu.VMEM((4,) + block, BF16)],
    )
    sums = keep + shift(send, "c", 1)
    sums = pick(sums, xl) + shift(pick(sums, 1 - xl), "xl", 1)
    col = sums[base : base + 3]
    mean_all = sums[base + 3] / 4
    between = sums[base + 5] / 4 - mean_all * mean_all
    var = sums[base + 4] / model + jnp.maximum(between, 0.0)
    rstd = lax.rsqrt(var + 1e-05)

    def normed(x, i, m, r):
        return ((x - m[:, None] * col[i][None, :]) * r[:, None]).astype(BF16)

    slab_of = lambda x: x.reshape(4, loc_dev)[:, :Q_DEV].reshape(-1)
    key_out = normed(sums[:n_rows], 0, mean_all, rstd)
    value_out = normed(sums[n_rows : 2 * n_rows], 1, mean_all, rstd)
    query_out = normed(sums[2 * n_rows : base], 2, slab_of(mean_all), slab_of(rstd))

    kv = jnp.concatenate([key_out, value_out], 1)
    kv_all = jnp.concatenate([kv, flip(kv, "z", 2), flip(kv, "z", 4), flip(kv, "z", 6)], 0)
    both = jnp.concatenate([query_out, flip(query_out, "z", 1)], 0)
    scores = factor * lax.dot_general(both, kv_all[:, :head_dim], NT, preferred_element_type=F32)
    top = jnp.max(scores, axis=-1, keepdims=True)
    powers = jnp.exp(scores - top)
    total = jnp.sum(powers, axis=-1, keepdims=True)
    part_out = jnp.dot(powers, kv_all[:, head_dim:].astype(F32), precision=lax.Precision.HIGHEST)
    half_lanes = (part_out.shape[0], head_dim // 2)
    ends = jnp.concatenate([part_out, jnp.broadcast_to(top, half_lanes), jnp.broadcast_to(total, half_lanes)], 1)
    ends = jnp.moveaxis(ends.reshape(2, 2, 2, Q_DEV, 2 * head_dim), 2, 0)
    ends = by_bit(c, pick(ends, c), shift(pick(ends, 1 - c), "c", 1))
    ends = jnp.moveaxis(ends, 2, 0)
    near, far = pick(ends, xl), pick(ends, 1 - xl)
    cross = [(x * n_z + i, (1 - x) * n_z + (i ^ 1)) for x in (0, 1) for i in range(n_z)]
    here = by_bit(xl, near[:, 0], shift(far[:, 0], "xl", 1))
    there = by_bit(xl, flip(near[:, 1], "z", 1), lax.ppermute(far[:, 1], ("xl", "z"), cross))
    tops = [e[..., head_dim : head_dim + 1] for e in (here, there)]
    best = jnp.maximum(*tops)
    scales = [jnp.exp(t - best) for t in tops]
    total = sum(f * e[..., -1:] for f, e in zip(scales, (here, there)))
    attended = sum(f * e[..., :head_dim] for f, e in zip(scales, (here, there))) / total
    return jnp.moveaxis(attended.reshape(heads, Q_DEV, head_dim), 1, 0).reshape(Q_DEV, columns).astype(BF16)


def solution(mesh):
    n_z = mesh.devices.shape[0] // 4
    fine = Mesh(mesh.devices.reshape(2, n_z, 2, 4, 2), WIDE + HEAD)
    placed = (
        P(WIDE, None, None),
        P(WIDE),
        P(HEAD),
        P(WIDE, HEAD),
        P(WIDE, HEAD),
        P(HEAD, WIDE),
        P(),
        P(WIDE, HEAD),
        P(WIDE, HEAD),
        P(WIDE, HEAD),
    )
    return jax.shard_map(on_device, mesh=fine, in_specs=placed, out_specs=P(WIDE, HEAD), check_vma=False)
```
